32 devices in a mesh: film: 2 (over y), site: 4 (over z), pair: 2 (over x), orb: 2 (over core).
Axes of the slice: x: 2, y: 2, z: 4, core: 2. Of those that a mesh axis runs over, the one named last changes fastest.
Arguments:
- coeff: bfloat16 [512, 16, 256], P(('film', 'site'), 'orb'), parts along dimension 0, may hold values from -0.375 to 0.375
- fock_pair: bfloat16 [512, 2, 256, 256], P(('film', 'site'), 'pair'), parts along dimension 0, may hold values from -6 to 6
- fock_site: bfloat16 [512, 256, 256], P(('film', 'site', 'pair')), parts along dimension 0, may hold values from -6 to 6
- pair_right: int32 [512, 2], P(('film', 'site'), 'pair'), parts along dimension 0, may hold values from -1 to 255, as said below
Outputs:
- coupling: float32 [512, 16, 4, 16], P(('film', 'site'), None, 'pair', 'orb'), parts along dimension 0
- site_energy: float32 [512, 16], P(('film', 'site', 'pair'), 'orb'), parts along dimension 0
The draws below stay inside these ranges and needn't reach their ends.
There are 2 independent parts, one for each index of `film`. The reference program is written for one: setup_inputs(seed, part) draws one part's arguments, and reference() takes and returns one part's arrays. A program takes and returns all parts, laid end to end along the dimension named above; each array names one. Nothing has to cross between parts.
Inputs may be any that keep to these rules, and one draw needn't show every extreme that they name: pair_right[m, q] is -1 (no pair in entry q) or the molecule paired with m there, never m itself; within one column q every molecule is named at most once; within one column, the 64 molecules of one site group name at most 16 molecules of any one site group.
All inputs are finite; a program needn't handle non-finite values.
Results may differ from the reference program's by a relative error of at most 0.0003.
Values may be sent and summed in bfloat16 or wider, within the bound.
A program may use at most 64 MiB of HBM per device.

```python
import jax
import jax.numpy as jnp
from jax import lax

NB = 256
NO = 16
MOL_SITE = 64
PAIR_DEV = 1
MOLS = 256
ENTRIES = 2
N_SITE = 4
N_PAIR = 2


def draw_pair_right(key, part):
    key = jax.random.fold_in(key, 11)
    level_key, full_key, column_key = jax.random.split(key, 3)
    levels = jax.random.randint(level_key, (N_PAIR,), 0, 4)
    fullest = jax.random.randint(full_key, (), 0, N_PAIR)
    levels = jnp.where(jnp.arange(N_PAIR) == fullest, 0, levels)
    limits = jnp.array([100, 50, 25, 12], jnp.int32)[levels]
    group_rows = jnp.arange(N_SITE)[:, None]
    local_rows = jnp.arange(MOL_SITE)[None, :]
    columns_out = []
    for column in range(N_PAIR * PAIR_DEV):
        own_key = jax.random.fold_in(column_key, column)
        group_key, local_key, live_key = jax.random.split(own_key, 3)
        relabel = jax.random.permutation(group_key, N_SITE)
        local_perm = jax.vmap(lambda sub: jax.random.permutation(sub, MOL_SITE))(jax.random.split(local_key, N_SITE))
        left_group = relabel[group_rows] + 0 * local_rows
        left_ids = left_group * MOL_SITE + local_perm[left_group, local_rows]
        right_group = relabel[(group_rows + local_rows) % N_SITE]
        right_ids = right_group * MOL_SITE + local_perm[right_group, (local_rows + 1) % MOL_SITE]
        table = jnp.zeros((MOLS,), jnp.int32).at[left_ids.reshape(-1)].set(right_ids.reshape(-1).astype(jnp.int32))
        chance = jax.random.randint(live_key, (MOLS,), 0, 100)
        columns_out.append(jnp.where(chance < limits[column // PAIR_DEV], table, -1))
    return jnp.stack(columns_out, axis=1).astype(jnp.int32)


def steps_of(key, shape, cuts, least, top_value):
    def one(position, shards_of):
        heights = jax.random.uniform(jax.random.fold_in(jax.random.fold_in(key, 6), position), (shards_of,), jnp.float32, least / len(cuts), top_value / len(cuts))
        return jnp.repeat(jnp.exp(heights), shape[position] // shards_of).reshape((-1,) + (1,) * (len(shape) - position - 1))

    level = one(*cuts[0])
    for cut in cuts[1:]:
        level = level * one(*cut)
    return level


def noise(stream_key, dims, scale, most, cuts=(), held_as=jnp.bfloat16):
    drawn = scale * jax.random.normal(stream_key, dims, jnp.float32)
    if cuts:
        drawn = drawn * steps_of(stream_key, dims, cuts, -0.22, 0.18)
    return jnp.clip(drawn, -most, most).astype(held_as)


def setup_inputs(seed: int = 0, part: int = 0) -> dict:
    streams_of = jax.random.split(jax.random.key(seed), 5)
    part_splits = jax.random.split(jax.random.fold_in(streams_of[4], part), 5)
    coeff = noise(part_splits[0], (MOLS, NO, NB), NB ** -0.5, 0.375, ((0, 4), (1, 2)))
    fock_pair = noise(part_splits[1], (MOLS, ENTRIES, NB, NB), 1.0, 6.0, ((0, 4), (1, 2)))
    fock_site = noise(part_splits[2], (MOLS, NB, NB), 1.0, 6.0, ((0, 8),))
    pair_right = draw_pair_right(jax.random.fold_in(jax.random.fold_in(streams_of[4], part), 71), part)
    return dict(coeff=coeff, fock_pair=fock_pair, fock_site=fock_site, pair_right=pair_right)


def reference(coeff, fock_pair, fock_site, pair_right):
    coeff_wide = coeff.astype(jnp.float32)
    is_live = pair_right >= 0
    partner = jnp.where(is_live, pair_right, 0).astype(jnp.int32)

    def one_molecule(pieces):
        left_panel, blocks, picked, usable = pieces
        spread = jnp.einsum('au,quv->qav', left_panel, blocks.astype(jnp.float32), precision=lax.Precision.HIGHEST)
        right_panels = coeff_wide[picked]
        product = jnp.einsum('qav,qbv->qab', spread, right_panels, precision=lax.Precision.HIGHEST)
        return jnp.where(usable[:, None, None], product, jnp.zeros_like(product))

    pair_block = lax.map(one_molecule, (coeff_wide, fock_pair, partner, is_live))
    target = jnp.where(is_live, pair_right, MOLS).astype(jnp.int32)
    columns = jnp.broadcast_to(jnp.arange(ENTRIES, dtype=jnp.int32)[None, :], target.shape)
    odd_slots = jnp.zeros((MOLS, ENTRIES, NO, NO), jnp.float32).at[target, columns].set(jnp.swapaxes(pair_block, 2, 3), mode="drop")
    joined = jnp.stack([pair_block, odd_slots], axis=2).reshape(MOLS, 2 * ENTRIES, NO, NO)
    coupling = jnp.transpose(joined, (0, 2, 1, 3))

    def own_energy(pieces):
        panel, block = pieces
        spread = jnp.dot(panel, block.astype(jnp.float32), precision=lax.Precision.HIGHEST)
        return jnp.sum(spread * panel, axis=1)

    site_energy = lax.map(own_energy, (coeff_wide, fock_site))
    return coupling, site_energy
```

```python
import functools

import jax
import jax.numpy as jnp
from jax import lax
from jax.experimental import pallas as pl
from jax.experimental.pallas import tpu as pltpu
from jax.sharding import PartitionSpec as P

F32 = jnp.float32
BF16 = jnp.bfloat16
STEP = 8
ROWS_LAST = (((1,), (1,)), ((), ()))
ROWS_FIRST = (((0,), (0,)), ((), ()))


def iota(shape, axis):
    return lax.broadcasted_iota(jnp.int32, shape, axis)


def as_bf16(flags):
    return jnp.where(flags, 1.0, 0.0).astype(BF16)


def two_parts(value):
    high = value.astype(BF16)
    return high, (value - high.astype(F32)).astype(BF16)


def pick_left(onehot, value):
    high, low = two_parts(value)
    return jnp.dot(onehot, high, preferred_element_type=F32) + jnp.dot(
        onehot, low, preferred_element_type=F32
    )


def pick_right(value, onehot):
    high, low = two_parts(value)
    return jnp.dot(high, onehot, preferred_element_type=F32) + jnp.dot(
        low, onehot, preferred_element_type=F32
    )


def kernel(
    sites, group, half, bucket, own,
    coeff_ref, pair_ref, site_ref, right_ref, out_ref, energy_ref,
    whole, blocks, own_blocks, rights, sent_panels, panels, image_high, image_low,
    pair_rows, payload, arrived,
    load_sem, block_sem, own_sem, orb_sems, right_sems, panel_sems, payload_sems,
):
    site = lax.axis_index("site")
    orb = lax.axis_index("orb")
    pair = lax.axis_index("pair")
    other = 1 - orb
    basis = whole.shape[2]
    panel = bucket * half
    slots = sites * bucket

    load = pltpu.make_async_copy(coeff_ref, whole.at[orb], load_sem)
    load.start()
    own_steps = own // STEP
    steps = group // STEP
    own_loads = []
    for step in range(own_steps):
        part = pl.ds(step * STEP, STEP)
        own_loads.append(pltpu.make_async_copy(site_ref.at[part], own_blocks.at[part], own_sem.at[step]))
        own_loads[-1].start()
    block_loads = []
    for step in range(steps):
        part = pl.ds(step * STEP, STEP)
        block_loads.append(pltpu.make_async_copy(pair_ref.at[part], blocks.at[part], block_sem.at[step]))
        block_loads[-1].start()

    barrier = pltpu.get_barrier_semaphore()
    for ahead in range(sites):
        to_site = lax.rem(site + ahead, sites)
        for cross in range(2):
            if ahead or cross:
                to_orb = other if cross else orb
                pl.semaphore_signal(
                    barrier, inc=1, device_id={"site": to_site, "orb": to_orb},
                    device_id_type=pl.DeviceIdType.MESH,
                )
    pl.semaphore_wait(barrier, 2 * sites - 1)

    right_sends = []
    for ahead in range(1, sites):
        right_sends.append(pltpu.make_async_remote_copy(
            src_ref=right_ref, dst_ref=rights.at[site],
            send_sem=right_sems.at[0, ahead], recv_sem=right_sems.at[1, ahead],
            device_id={"site": lax.rem(site + ahead, sites)},
            device_id_type=pl.DeviceIdType.MESH,
        ))
        right_sends[-1].start()
    orb_send = pltpu.make_async_remote_copy(
        src_ref=coeff_ref, dst_ref=whole.at[orb],
        send_sem=orb_sems.at[0], recv_sem=orb_sems.at[1],
        device_id={"orb": other}, device_id_type=pl.DeviceIdType.MESH,
    )
    orb_send.start()

    rights[site] = right_ref[...]
    upper = as_bf16(iota((group, group), 0) < iota((group, group), 1))
    mine = right_ref[...]
    site_row = iota((sites, group), 0)
    named = (mine >= site_row * group) & (mine < site_row * group + group)
    rank = jnp.dot(as_bf16(named), upper, preferred_element_type=F32).astype(jnp.int32)
    place = jnp.sum(jnp.where(named, site_row * bucket + rank + 1, 0), axis=0, keepdims=True) - 1

    load.wait()
    for send in right_sends:
        send.wait_recv()
    wanted = [None] * sites
    for source in range(sites):
        theirs = rights[source]
        asked = (theirs >= site * group) & (theirs < site * group + group)
        order = jnp.dot(
            as_bf16(jnp.broadcast_to(asked, (8, group))), upper, preferred_element_type=F32
        )[0:1].astype(jnp.int32)
        order = jnp.where(asked, order, -1)
        hit = order == iota((bucket, group), 0)
        local = jnp.sum(jnp.where(hit, theirs - site * group + 1, 0), axis=1, keepdims=True) - 1
        wanted[source] = local
        hit_rows = order == (iota((panel, group), 0) >> 3)
        local_rows = jnp.sum(jnp.where(hit_rows, theirs - site * group + 1, 0), axis=1, keepdims=True) - 1
        row = jnp.where(local_rows >= 0, local_rows * half + (iota((panel, 1), 0) & 7), -1)
        onehot = as_bf16(row == iota((panel, group * half), 1))
        sent_panels[source] = jnp.dot(
            onehot, whole[orb], preferred_element_type=F32
        ).astype(BF16)

    panel_sends = []
    for ahead in range(1, sites):
        to_site = lax.rem(site + ahead, sites)
        panel_sends.append(pltpu.make_async_remote_copy(
            src_ref=sent_panels.at[to_site], dst_ref=panels.at[site],
            send_sem=panel_sems.at[0, ahead], recv_sem=panel_sems.at[1, ahead],
            device_id={"site": to_site}, device_id_type=pl.DeviceIdType.MESH,
        ))
        panel_sends[-1].start()
    panels[site] = sent_panels[site]

    energy = jnp.zeros((half, own), F32)
    lane = iota((half, own), 1)
    for step in range(own_steps):
        own_loads[step].wait()
        for two in range(STEP // 2):
            first = step * STEP + 2 * two
            start = pl.multiple_of((pair * own + first) * half, 2 * half)
            left = whole[orb, pl.ds(start, 2 * half), :]
            wide = left.astype(F32)
            for odd in range(2):
                spread = jnp.dot(left, own_blocks[first + odd], preferred_element_type=F32)
                part = slice(odd * half, (odd + 1) * half)
                total = jnp.sum(spread[part] * wide[part], axis=1, keepdims=True)
                energy = jnp.where(lane == first + odd, total, energy)
    energy_ref[...] = energy

    orb_send.wait_recv()
    for step in range(steps):
        block_loads[step].wait()
        for two in range(STEP // 2):
            first = step * STEP + 2 * two
            rows = pl.ds(first * half, 2 * half)
            left = jnp.concatenate([whole[0, rows, :], whole[1, rows, :]], axis=0)
            one = jnp.dot(left, blocks[first], preferred_element_type=F32)
            nxt = jnp.dot(left, blocks[first + 1], preferred_element_type=F32)
            image = jnp.concatenate(
                [one[:half], nxt[half : 2 * half], one[2 * half : 3 * half], nxt[3 * half :]], axis=0
            )
            high, low = two_parts(image)
            to = pl.ds(first * 2 * half, 4 * half)
            image_high[to, :] = high
            image_low[to, :] = low

    entry_row = iota((group * half, group), 0) >> 3
    place_col = jnp.sum(
        jnp.where(entry_row == iota((group * half, group), 1), place + 1, 0), axis=1, keepdims=True
    ) - 1
    source_row = jnp.where(place_col >= 0, place_col * half + (iota((group * half, 1), 0) & 7), -1)
    reorder = as_bf16(source_row == iota((group * half, slots * half), 1))
    pack = as_bf16(place == iota((slots, group), 0))
    unpack = as_bf16(jnp.concatenate(wanted, axis=0) == iota((slots, group), 1))

    few = basis // half
    rows = few * 2 * half
    row = iota((rows, few * half), 0)
    row_entry = ((row >> 5) << 1) + ((row >> 3) & 1)
    same_entry = row_entry == (iota((rows, few * half), 1) >> 3)
    width = 2 * half * half
    fold = as_bf16((iota((few * half, width), 0) & 7) == ((iota((few * half, width), 1) >> 3) & 7))
    row = iota((rows, width), 0)
    col = iota((rows, width), 1)
    same_orb = (((row >> 4) & 1) == (col >> 6)) & ((row & 7) == (col & 7))
    row = iota((few, rows), 1)
    gather = as_bf16(((row >> 5) << 1) + ((row >> 3) & 1) == iota((few, rows), 0))

    for send in panel_sends:
        send.wait_recv()
    right = jnp.dot(
        reorder, panels[...].reshape(slots * half, basis), preferred_element_type=F32
    ).astype(BF16)
    parts = []
    for index in range(group // few):
        part = right[index * few * half : (index + 1) * few * half]
        span = pl.ds(index * rows, rows)
        full = lax.dot_general(image_high[span, :], part, ROWS_LAST, preferred_element_type=F32)
        full += lax.dot_general(image_low[span, :], part, ROWS_LAST, preferred_element_type=F32)
        folded = pick_right(jnp.where(same_entry, full, 0.0), fold)
        parts.append(pick_left(gather, jnp.where(same_orb, folded, 0.0)))
    by_entry = jnp.concatenate(parts, axis=0)
    payload[...] = pick_left(pack, by_entry).reshape(sites, bucket, width)

    payload_sends = []
    for ahead in range(sites):
        to_site = lax.rem(site + ahead, sites)
        for cross in range(2):
            if ahead or cross:
                payload_sends.append(pltpu.make_async_remote_copy(
                    src_ref=payload.at[to_site], dst_ref=arrived.at[orb, site],
                    send_sem=payload_sems.at[0, 2 * ahead + cross],
                    recv_sem=payload_sems.at[1, 2 * ahead + cross],
                    device_id={"site": to_site, "orb": other if cross else orb},
                    device_id_type=pl.DeviceIdType.MESH,
                ))
                payload_sends[-1].start()
    arrived[orb, site] = payload[site]

    pair_rows[...] = by_entry.T
    for a in range(2 * half):
        start = (a // half) * half * half + a % half
        out_ref[pl.ds(a * 2 * half, half), :] = pair_rows[pl.ds(start, half, stride=half), :]

    for send in payload_sends:
        send.wait_recv()
    for b_half in range(2):
        high, low = two_parts(arrived[b_half].reshape(slots, width))
        moved = lax.dot_general(high, unpack, ROWS_FIRST, preferred_element_type=F32)
        moved += lax.dot_general(low, unpack, ROWS_FIRST, preferred_element_type=F32)
        moved = jnp.where(orb == 0, moved[: half * half], moved[half * half :])
        for b in range(half):
            to = (b_half * half + b) * 2 * half + half
            out_ref[pl.ds(to, half), :] = moved[b * half : (b + 1) * half]

    for send in right_sends + [orb_send] + panel_sends + payload_sends:
        send.wait_send()


def local(sites, coeff, fock_pair, fock_site, pair_right):
    group, half, basis = coeff.shape
    own = fock_site.shape[0]
    bucket = -(-(group // sites) // 8) * 8
    width = 2 * half * half
    dma = pltpu.SemaphoreType.DMA
    any_space = pl.BlockSpec(memory_space=pl.ANY)
    vmem = pl.BlockSpec(memory_space=pltpu.VMEM)
    coupling, energy = pl.pallas_call(
        functools.partial(kernel, sites, group, half, bucket, own),
        out_shape=(
            jax.ShapeDtypeStruct((4 * half * half, group), F32),
            jax.ShapeDtypeStruct((half, own), F32),
        ),
        in_specs=[any_space, any_space, any_space, vmem],
        out_specs=(vmem, vmem),
        scratch_shapes=[
            pltpu.VMEM((2, group * half, basis), BF16),
            pltpu.VMEM((group, basis, basis), BF16),
            pltpu.VMEM((own, basis, basis), BF16),
            pltpu.VMEM((sites, 1, group), jnp.int32),
            pltpu.VMEM((sites, bucket * half, basis), BF16),
            pltpu.VMEM((sites, bucket * half, basis), BF16),
            pltpu.VMEM((group * 2 * half, basis), BF16),
            pltpu.VMEM((group * 2 * half, basis), BF16),
            pltpu.VMEM((width, group), F32),
            pltpu.VMEM((sites, bucket, width), F32),
            pltpu.VMEM((2, sites, bucket, width), F32),
            dma,
            dma((group // STEP,)),
            dma((own // STEP,)),
            dma((2,)),
            dma((2, sites)),
            dma((2, sites)),
            dma((2, 2 * sites)),
        ],
        compiler_params=pltpu.CompilerParams(
            collective_id=0, has_side_effects=True, vmem_limit_bytes=48 * 2**20
        ),
    )(
        coeff.reshape(group * half, basis),
        fock_pair.reshape(group, basis, basis),
        fock_site,
        pair_right.reshape(1, group),
    )
    coupling = coupling.reshape(2 * half, 2, half, group).transpose(3, 0, 1, 2)
    return coupling, energy.T


def solution(mesh):
    return jax.shard_map(
        functools.partial(local, mesh.shape["site"]),
        mesh=mesh,
        in_specs=(
            P(("film", "site"), "orb", None),
            P(("film", "site"), "pair", None, None),
            P(("film", "site", "pair"), None, None),
            P(("film", "site"), "pair"),
        ),
        out_specs=(P(("film", "site"), None, "pair", "orb"), P(("film", "site", "pair"), "orb")),
        check_vma=False,
    )
```

```python
import functools

import jax
import jax.numpy as jnp
from jax import lax
from jax.experimental import pallas as pl
from jax.experimental.pallas import tpu as pltpu
from jax.sharding import PartitionSpec as P

F32 = jnp.float32
BF16 = jnp.bfloat16
STEP = 8
ROWS_LAST = (((1,), (1,)), ((), ()))
ROWS_FIRST = (((0,), (0,)), ((), ()))


def iota(shape, axis):
    return lax.broadcasted_iota(jnp.int32, shape, axis)


def as_bf16(flags):
    return jnp.where(flags, 1.0, 0.0).astype(BF16)


def two_parts(value):
    high = value.astype(BF16)
    return high, (value - high.astype(F32)).astype(BF16)


def pick_left(onehot, value):
    high, low = two_parts(value)
    return jnp.dot(onehot, high, preferred_element_type=F32) + jnp.dot(
        onehot, low, preferred_element_type=F32
    )


def pick_right(value, onehot):
    high, low = two_parts(value)
    return jnp.dot(high, onehot, preferred_element_type=F32) + jnp.dot(
        low, onehot, preferred_element_type=F32
    )


def peer_of(site, turn):
    peer, bit = site, 1
    while bit <= turn:
        if turn & bit:
            peer = peer + bit - 2 * bit * lax.rem(lax.div(peer, bit), 2)
        bit *= 2
    return peer


def kernel(
    sites, group, half, bucket, own,
    coeff_ref, pair_ref, site_ref, right_ref, out_ref,
    whole, blocks, own_blocks, rights, sent_panels, panels, image, ordered,
    pair_rows, payload, arrived,
    load_sem, mine_sem, block_sem, own_sem, orb_sems, right_sems, panel_sems, payload_sems,
):
    site = lax.axis_index("site")
    orb = lax.axis_index("orb")
    pair = lax.axis_index("pair")
    other = 1 - orb
    basis = whole.shape[2]
    panel = bucket * half
    slots = sites * bucket
    orbs = 2 * half
    rows = bucket * orbs
    peers = [peer_of(site, turn) for turn in range(sites)]

    mine_load = pltpu.make_async_copy(right_ref, rights.at[0], mine_sem)
    mine_load.start()
    load = pltpu.make_async_copy(coeff_ref, whole.at[orb], load_sem)
    load.start()
    barrier = pltpu.get_barrier_semaphore()
    for turn in range(sites):
        for cross in range(2):
            if turn or cross:
                pl.semaphore_signal(
                    barrier, inc=1,
                    device_id={"site": peers[turn], "orb": other if cross else orb},
                    device_id_type=pl.DeviceIdType.MESH,
                )
    own_steps = own // STEP
    steps = group // STEP
    own_loads = []
    for step in range(own_steps):
        part = pl.ds(step * STEP, STEP)
        own_loads.append(pltpu.make_async_copy(site_ref.at[part], own_blocks.at[part], own_sem.at[step]))
        own_loads[-1].start()
    block_loads = []
    for step in range(steps):
        part = pl.ds(step * STEP, STEP)
        block_loads.append(pltpu.make_async_copy(pair_ref.at[part], blocks.at[part], block_sem.at[step]))
        block_loads[-1].start()

    upper = as_bf16(iota((group, group), 0) < iota((group, group), 1))
    mine_load.wait()
    mine = rights[0]
    pl.semaphore_wait(barrier, 2 * sites - 1)

    right_sends = []
    for turn in reversed(range(1, sites)):
        right_sends.append(pltpu.make_async_remote_copy(
            src_ref=rights.at[0], dst_ref=rights.at[turn],
            send_sem=right_sems.at[0, turn], recv_sem=right_sems.at[1, turn],
            device_id={"site": peers[turn]}, device_id_type=pl.DeviceIdType.MESH,
        ))
        right_sends[-1].start()
    orb_send = pltpu.make_async_remote_copy(
        src_ref=coeff_ref, dst_ref=whole.at[orb],
        send_sem=orb_sems.at[0], recv_sem=orb_sems.at[1],
        device_id={"orb": other}, device_id_type=pl.DeviceIdType.MESH,
    )
    orb_send.start()

    peer_row = jnp.zeros((sites, group), jnp.int32)
    for turn in range(sites):
        peer_row = jnp.where(iota((sites, group), 0) == turn, peers[turn], peer_row)
    named = (mine >= peer_row * group) & (mine < peer_row * group + group)
    rank = jnp.dot(as_bf16(named), upper, preferred_element_type=F32).astype(jnp.int32)
    place = jnp.sum(
        jnp.where(named, iota((sites, group), 0) * bucket + rank + 1, 0), axis=0, keepdims=True
    ) - 1

    load.wait()
    for send in right_sends:
        send.wait_recv()
    theirs = jnp.concatenate([rights[turn] for turn in range(sites)], axis=0)
    asked = (theirs >= site * group) & (theirs < site * group + group)
    orders = jnp.dot(as_bf16(asked), upper, preferred_element_type=F32).astype(jnp.int32)
    orders = jnp.where(asked, orders, -1)
    wanted = [None] * sites
    panel_sends = []
    for turn in reversed(range(sites)):
        order = orders[turn : turn + 1]
        found = rights[turn] - site * group + 1
        hit = order == (iota((panel, group), 0) >> 3)
        local_rows = jnp.sum(jnp.where(hit, found, 0), axis=1, keepdims=True) - 1
        row = jnp.where(local_rows >= 0, local_rows * half + (iota((panel, 1), 0) & 7), -1)
        onehot = as_bf16(row == iota((panel, group * half), 1))
        picked = jnp.dot(onehot, whole[orb], preferred_element_type=F32).astype(BF16)
        if turn:
            sent_panels[turn] = picked
            panel_sends.append(pltpu.make_async_remote_copy(
                src_ref=sent_panels.at[turn], dst_ref=panels.at[turn],
                send_sem=panel_sems.at[0, turn], recv_sem=panel_sems.at[1, turn],
                device_id={"site": peers[turn]}, device_id_type=pl.DeviceIdType.MESH,
            ))
            panel_sends[-1].start()
        else:
            panels[0] = picked
    for turn in range(sites):
        hit = orders[turn : turn + 1] == iota((bucket, group), 0)
        found = rights[turn] - site * group + 1
        wanted[turn] = jnp.sum(jnp.where(hit, found, 0), axis=1, keepdims=True) - 1

    orb_send.wait_recv()
    for step in range(steps):
        block_loads[step].wait()
        for two in range(STEP // 2):
            first = step * STEP + 2 * two
            part = pl.ds(first * half, orbs)
            left = jnp.concatenate([whole[0, part, :], whole[1, part, :]], axis=0)
            one = jnp.dot(left, blocks[first], preferred_element_type=F32)
            nxt = jnp.dot(left, blocks[first + 1], preferred_element_type=F32)
            joined = jnp.concatenate(
                [one[:half], nxt[half : 2 * half], one[2 * half : 3 * half], nxt[3 * half :]], axis=0
            )
            high, low = two_parts(joined)
            to = pl.ds(first * orbs, 2 * orbs)
            image[to, :basis] = high
            image[to, basis:] = low

    total_rows = group * orbs
    row = iota((group, total_rows), 1)
    spread_row = as_bf16(((row >> 5) << 1) + ((row >> 3) & 1) == iota((group, total_rows), 0))
    row = iota((1, total_rows), 1)
    key = jnp.dot(
        jnp.broadcast_to(place, (8, group)).astype(F32).astype(BF16), spread_row,
        preferred_element_type=F32,
    )[0:1].astype(jnp.int32)
    key = jnp.where(key >= 0, key * orbs + ((row >> 4) & 1) * half + (row & 7), -1)
    for turn in range(sites):
        onehot = as_bf16(key == iota((rows, total_rows), 0) + turn * rows)
        both = jnp.dot(onehot, image[...], preferred_element_type=F32).astype(BF16)
        ordered[turn, :rows, :] = both[:, :basis]
        ordered[turn, rows:, :] = both[:, basis:]

    energy = jnp.zeros((half, own), F32)
    lane = iota((half, own), 1)
    for step in range(own_steps):
        own_loads[step].wait()
        for two in range(STEP // 2):
            first = step * STEP + 2 * two
            start = pl.multiple_of((pair * own + first) * half, orbs)
            left = whole[orb, pl.ds(start, orbs), :]
            wide = left.astype(F32)
            for odd in range(2):
                spread = jnp.dot(left, own_blocks[first + odd], preferred_element_type=F32)
                part = slice(odd * half, (odd + 1) * half)
                total = jnp.sum(spread[part] * wide[part], axis=1, keepdims=True)
                energy = jnp.where(lane == first + odd, total, energy)
    out_ref[pl.ds(4 * half * half, half), pl.ds(0, own)] = energy

    pack = as_bf16(place == iota((slots, group), 0))
    unpack = as_bf16(jnp.concatenate(wanted, axis=0) == iota((slots, group), 1))
    same_slot = (iota((rows, panel), 0) >> 4) == (iota((rows, panel), 1) >> 3)
    width = 2 * half * half
    fold = as_bf16((iota((panel, width), 0) & 7) == ((iota((panel, width), 1) >> 3) & 7))
    row = iota((rows, width), 0)
    col = iota((rows, width), 1)
    same_orb = ((row >> 3) & 1 == (col >> 6)) & ((row & 7) == (col & 7))

    waits = {turn: send for turn, send in zip(reversed(range(1, sites)), panel_sends)}
    payload_sends = []
    for turn in range(sites):
        if turn:
            waits[turn].wait_recv()
        full = lax.dot_general(ordered[turn], panels[turn], ROWS_LAST, preferred_element_type=F32)
        full = jnp.where(same_slot, full[:rows] + full[rows:], 0.0)
        folded = jnp.where(same_orb, pick_right(full, fold), 0.0)
        payload[turn] = jnp.sum(folded.reshape(bucket, orbs, width), axis=1)
        for cross in range(2):
            if turn or cross:
                payload_sends.append(pltpu.make_async_remote_copy(
                    src_ref=payload.at[turn], dst_ref=arrived.at[orb, turn],
                    send_sem=payload_sems.at[0, 2 * turn + cross],
                    recv_sem=payload_sems.at[1, 2 * turn + cross],
                    device_id={"site": peers[turn], "orb": other if cross else orb},
                    device_id_type=pl.DeviceIdType.MESH,
                ))
                payload_sends[-1].start()
    arrived[orb, 0] = payload[0]

    high, low = two_parts(payload[...].reshape(slots, width))
    by_entry = lax.dot_general(high, pack, ROWS_FIRST, preferred_element_type=F32)
    by_entry += lax.dot_general(low, pack, ROWS_FIRST, preferred_element_type=F32)
    pair_rows[...] = by_entry
    for a in range(orbs):
        start = (a // half) * half * half + a % half
        out_ref[pl.ds(a * orbs, half), :] = pair_rows[pl.ds(start, half, stride=half), :]

    for send in payload_sends:
        send.wait_recv()
    for b_half in range(2):
        high, low = two_parts(arrived[b_half].reshape(slots, width))
        moved = lax.dot_general(high, unpack, ROWS_FIRST, preferred_element_type=F32)
        moved += lax.dot_general(low, unpack, ROWS_FIRST, preferred_element_type=F32)
        moved = jnp.where(orb == 0, moved[: half * half], moved[half * half :])
        for b in range(half):
            to = (b_half * half + b) * orbs + half
            out_ref[pl.ds(to, half), :] = moved[b * half : (b + 1) * half]

    for send in right_sends + [orb_send] + panel_sends + payload_sends:
        send.wait_send()


def local(sites, coeff, fock_pair, fock_site, pair_right):
    group, half, basis = coeff.shape
    own = fock_site.shape[0]
    bucket = -(-(group // sites) // 8) * 8
    width = 2 * half * half
    dma = pltpu.SemaphoreType.DMA
    hbm = pl.BlockSpec(memory_space=pltpu.HBM)
    vmem = pl.BlockSpec(memory_space=pltpu.VMEM)
    joined = pl.pallas_call(
        functools.partial(kernel, sites, group, half, bucket, own),
        out_shape=jax.ShapeDtypeStruct((4 * half * half + half, group), F32),
        in_specs=[hbm] * 4,
        out_specs=vmem,
        scratch_shapes=[
            pltpu.VMEM((2, group * half, basis), BF16),
            pltpu.VMEM((group, basis, basis), BF16),
            pltpu.VMEM((own, basis, basis), BF16),
            pltpu.VMEM((sites, 1, group), jnp.int32),
            pltpu.VMEM((sites, bucket * half, basis), BF16),
            pltpu.VMEM((sites, bucket * half, basis), BF16),
            pltpu.VMEM((group * 2 * half, 2 * basis), BF16),
            pltpu.VMEM((sites, 2 * bucket * 2 * half, basis), BF16),
            pltpu.VMEM((width, group), F32),
            pltpu.VMEM((sites, bucket, width), F32),
            pltpu.VMEM((2, sites, bucket, width), F32),
            dma,
            dma,
            dma((group // STEP,)),
            dma((own // STEP,)),
            dma((2,)),
            dma((2, sites)),
            dma((2, sites)),
            dma((2, 2 * sites)),
        ],
        compiler_params=pltpu.CompilerParams(
            collective_id=0, has_side_effects=True, vmem_limit_bytes=53 * 2**20
        ),
    )(
        coeff.reshape(group * half, basis),
        fock_pair.reshape(group, basis, basis),
        fock_site,
        pair_right.reshape(1, group),
    )
    coupling, energy = joined[: 4 * half * half], joined[4 * half * half :, :own]
    coupling = coupling.reshape(2 * half, 2, half, group).transpose(3, 0, 1, 2)
    return coupling, energy.T


def solution(mesh):
    return jax.shard_map(
        functools.partial(local, mesh.shape["site"]),
        mesh=mesh,
        in_specs=(
            P(("film", "site"), "orb", None),
            P(("film", "site"), "pair", None, None),
            P(("film", "site", "pair"), None, None),
            P(("film", "site"), "pair"),
        ),
        out_specs=(P(("film", "site"), None, "pair", "orb"), P(("film", "site", "pair"), "orb")),
        check_vma=False,
    )
```
